32 devices in a mesh: grp: 2 (over x), section: 16 (over z, y, core).
Axes of the slice: x: 2, y: 2, z: 4, core: 2. Of those that a mesh axis runs over, the one named last changes fastest.
Arguments:
- latent: bfloat16 [1536, 64], P(('grp', 'section')), parts along dimension 0, may hold values from -6 to 6
- control_latent: bfloat16 [1536, 64], P(('grp', 'section')), parts along dimension 0, may hold values from -6 to 6
- patch_tiles: int32 [4], replicated, may hold values from 1 to 2, 6 in all
- tile_lists: int32 [2, 6, 3], replicated, may hold values from 0 to 5, as said below
- tile_counts: int32 [2, 6], replicated, may hold values from 1 to 3, as said below
- embed_weight: bfloat16 [64, 3072], replicated, may hold values from -0.75 to 0.75
- control_embed: bfloat16 [64, 3072], replicated, may hold values from -0.75 to 0.75
- modulation: float32 [2, 3, 3072], replicated, may hold values from -4 to 4
- qk_gain: float32 [2, 2, 128], replicated, may hold values from 0.1 to 1.9
- qkv_weight: bfloat16 [16, 3072, 1152], P('section'), may hold values from -0.109375 to 0.109375
- out_weight: bfloat16 [16, 384, 3072], P('section'), may hold values from -0.109375 to 0.109375
- stale_cache: bfloat16 [16, 1536, 768], P('section', 'grp'), parts along dimension 1, may hold values from -6 to 6
- control_gain: float32 [1, 3072], replicated, may hold values from -3 to 3
- final_mod: float32 [2, 3072], replicated, may hold values from -3 to 3
- final_weight: bfloat16 [3072, 64], replicated, may hold values from -0.109375 to 0.109375
Outputs:
- denoised: float32 [1536, 64], P(('grp', 'section')), parts along dimension 0
The draws below stay inside these ranges and needn't reach their ends.
There are 2 independent parts, one for each index of `grp`. The reference program is written for one: setup_inputs(seed, part) draws one part's arguments, and reference() takes and returns one part's arrays. A program takes and returns all parts, laid end to end along the dimension named above; an argument that names none is the same for every part. Nothing has to cross between parts.
Inputs may be any that keep to these rules, and one draw needn't show every extreme that they name: `patch_tiles`: the patches are contiguous and in order and together cover all 6 tiles; the largest has exactly 2 tiles. Entry 0 of tile_lists[b, t] is t itself; the 3 entries of one row are distinct. `tile_counts`: in every block slot some query tile uses all 3 listed tiles.
All inputs are finite; a program needn't handle non-finite values.
Results may differ from the reference program's by a relative error of at most 0.014.
Values may be sent and summed in bfloat16 or wider, within the bound.
A program may use at most 64 MiB of HBM per device.

```python
import math
import jax
import jax.numpy as jnp
import numpy as np
from jax import lax

D = 3072
HEADS = 24
HD = 128
HG = 8
HEADS_DEV = 3
C_OUT = 64
TILE = 128
KSEL = 3
PATCHES = 4
TILES = 6
PMAX = 2
SEQ = 768
SLOTS = 2
CTRL = 1
MAIN = 1


def draw_tile_lists(key, part):
    random_part = jax.random.randint(jax.random.fold_in(key, 11), (SLOTS, TILES, TILES), 0, 2 ** 18)
    tile_ids = jnp.arange(TILES, dtype=jnp.int32)
    distance = jnp.abs(tile_ids[:, None] - tile_ids[None, :])
    ranking = (random_part + distance[None, :, :] * 2 ** 16) * TILES + tile_ids[None, None, :]
    ranking = jnp.where(distance[None, :, :] == 0, -1, ranking)
    ordering = jnp.argsort(ranking, axis=-1, stable=True)
    return ordering[:, :, :KSEL].astype(jnp.int32)


def draw_tile_counts(key, part):
    drawn = jax.random.randint(jax.random.fold_in(key, 21), (SLOTS, TILES), 1, KSEL + 1)
    forced = jax.random.randint(jax.random.fold_in(key, 22), (SLOTS, 1), 0, TILES)
    tile_ids = jnp.arange(TILES, dtype=jnp.int32)[None, :]
    return jnp.where(tile_ids == forced, KSEL, drawn).astype(jnp.int32)


def levels(key, shape, cuts, low, high):
    loudness = 1.0
    for dim, shards_of in cuts:
        draws = jax.random.uniform(jax.random.fold_in(jax.random.fold_in(key, 6), dim), (shards_of,), jnp.float32, low / len(cuts), high / len(cuts))
        loudness = loudness * jnp.repeat(jnp.exp(draws), shape[dim] // shards_of).reshape((-1,) + (1,) * (len(shape) - 1 - dim))
    return loudness


def profile(number_of, total, limit, slope):
    loads = [(1 << 20) // math.isqrt(rank ** slope) + 1 for rank in range(2, number_of + 1)]
    surplus, counts = total - limit - (number_of - 1), [1] * (number_of - 1)
    while surplus > 0:
        free = [i for i in range(number_of - 1) if counts[i] < limit]
        mass, remaining = sum([loads[i] for i in free]), surplus
        for i in free:
            more = min(limit - counts[i], max(1, remaining * loads[i] // mass), surplus)
            counts[i] = counts[i] + more
            surplus = surplus - more
    return np.array([limit] + counts)


def ragged_sizes(rng, count, total, reach, skew):
    if count == 2:
        one = jax.random.randint(rng, (), max(1, total - reach), min(reach, total - 1) + 1)
        return jnp.stack([one, total - one])
    tallies = jnp.asarray(profile(count, total, reach, skew), jnp.int32)
    pairs = (count - 1) // 2
    source_of, sink = tallies[1:1 + 2 * pairs:2], tallies[2:2 + 2 * pairs:2]
    room = jnp.minimum(source_of - 1, reach - sink)
    shifted = jax.random.randint(jax.random.fold_in(rng, 1), (pairs,), 0, 1 << 20) % (room + 1)
    tallies = tallies.at[1:1 + 2 * pairs:2].set(source_of - shifted).at[2:2 + 2 * pairs:2].set(sink + shifted)
    return tallies[jax.random.permutation(jax.random.fold_in(rng, 2), count)]


def centred(stream_key, shape, spread, bound, split=(), kind=jnp.bfloat16):
    values = jax.random.normal(stream_key, shape, jnp.float32) * spread
    if len(split) > 0:
        values = levels(stream_key, shape, split, -0.22, 0.18) * values
    return jnp.clip(values, min=-bound, max=bound).astype(kind)


def setup_inputs(seed: int = 0, part: int = 0) -> dict:
    key_list = jax.random.split(jax.random.key(seed), 16)
    part_splits = jax.random.split(jax.random.fold_in(key_list[15], part), 16)
    return {
        "latent": centred(part_splits[0], (SEQ, C_OUT), 1.0, 6.0, ((0, 16),)),
        "control_latent": centred(part_splits[1], (SEQ, C_OUT), 1.0, 6.0, ((0, 16),)),
        "patch_tiles": ragged_sizes(key_list[2], PATCHES, TILES, PMAX, 0).astype(jnp.int32),
        "tile_lists": draw_tile_lists(jax.random.fold_in(key_list[15], 71), part),
        "tile_counts": draw_tile_counts(jax.random.fold_in(key_list[15], 71), part),
        "embed_weight": centred(key_list[5], (C_OUT, D), C_OUT ** -0.5, 0.75),
        "control_embed": centred(key_list[6], (C_OUT, D), C_OUT ** -0.5, 0.75),
        "modulation": centred(key_list[7], (SLOTS, 3, D), 1.0, 4.0, (), jnp.float32),
        "qk_gain": jnp.clip(1.0 + 0.18 * jax.random.normal(key_list[8], (SLOTS, 2, HD), jnp.float32), 0.1, 1.9),
        "qkv_weight": centred(key_list[9], (SLOTS * HG, D, 3 * HEADS_DEV * HD), D ** -0.5, 0.109375, ((0, 16),)),
        "out_weight": centred(key_list[10], (SLOTS * HG, HEADS_DEV * HD, D), (HEADS * HD) ** -0.5, 0.109375, ((0, 16),)),
        "stale_cache": centred(part_splits[11], (SLOTS * HG, SEQ, 2 * HEADS_DEV * HD), 1.0, 6.0, ((0, 16),)),
        "control_gain": centred(key_list[12], (CTRL, D), 0.5, 3.0, (), jnp.float32),
        "final_mod": centred(key_list[13], (2, D), 0.5, 3.0, (), jnp.float32),
        "final_weight": centred(key_list[14], (D, C_OUT), D ** -0.5, 0.109375),
    }


EPSILON = 1e-06

def modulated(hidden, shift_row, scale_row):
    values = hidden.astype(jnp.float32)
    centered = values - lax.optimization_barrier(jnp.mean(values, axis=-1, keepdims=True))
    variance = lax.optimization_barrier(jnp.mean(centered * centered, axis=-1, keepdims=True))
    normed = centered * lax.rsqrt(variance + EPSILON)
    return (normed * (1.0 + scale_row) + shift_row).astype(jnp.bfloat16)

def rms_scaled(values, gain_row):
    return values * lax.rsqrt(lax.optimization_barrier(jnp.mean(values * values, axis=-1, keepdims=True)) + EPSILON) * gain_row

def attend_group(modded, w_qkv, w_out, memory, gain_pair, start_tile, patch_length, tile_list, tile_limit):
    row_count = modded.shape[0]
    query_tiles_count = row_count // TILE
    head_count = w_out.shape[0] // HD
    projected = jnp.dot(modded, w_qkv, preferred_element_type=jnp.float32).reshape(row_count, 3, head_count, HD)
    queries = rms_scaled(projected[:, 0], gain_pair[0]).astype(jnp.bfloat16)
    keys_new = rms_scaled(projected[:, 1], gain_pair[1]).astype(jnp.bfloat16)
    values_new = projected[:, 2].astype(jnp.bfloat16)
    fresh_rows = jnp.concatenate([keys_new.reshape(row_count, head_count * HD), values_new.reshape(row_count, head_count * HD)], axis=1)
    row_start = (start_tile * TILE).astype(jnp.int32)
    previous = lax.dynamic_slice_in_dim(memory, row_start, row_count, 0)
    live_rows = jnp.arange(row_count) < patch_length * TILE
    memory = lax.dynamic_update_slice_in_dim(memory, jnp.where(live_rows[:, None], fresh_rows, previous), row_start, 0)
    tiled_memory = memory.reshape(-1, TILE, 2, head_count, HD)
    query_tiles = jnp.minimum(start_tile + jnp.arange(query_tiles_count), TILES - 1).astype(jnp.int32)
    picked = tile_list[query_tiles]
    used_counts = tile_limit[query_tiles]
    chosen = tiled_memory[picked]
    key_rows = chosen[:, :, :, 0].reshape(query_tiles_count, KSEL * TILE, head_count, HD)
    value_rows = chosen[:, :, :, 1].reshape(query_tiles_count, KSEL * TILE, head_count, HD)
    query_rows = queries.reshape(query_tiles_count, TILE, head_count, HD)
    scores = jnp.einsum('tqhd,tkhd->thqk', query_rows.astype(jnp.float32), key_rows.astype(jnp.float32)) / math.sqrt(HD)
    allowed = (jnp.arange(KSEL * TILE) // TILE)[None, :] < used_counts[:, None]
    scores = jnp.where(allowed[:, None, None, :], scores, -1e+30)
    highest = lax.optimization_barrier(jnp.max(scores, axis=-1, keepdims=True))
    weights = jnp.exp(scores - highest)
    probabilities = (weights / lax.optimization_barrier(jnp.sum(weights, axis=-1, keepdims=True))).astype(jnp.bfloat16)
    attended = jnp.einsum('thqk,tkhd->tqhd', probabilities.astype(jnp.float32), value_rows.astype(jnp.float32)).astype(jnp.bfloat16)
    attended = attended.reshape(row_count, head_count * HD)
    partial_value = jnp.dot(attended, w_out, preferred_element_type=jnp.float32)
    return (partial_value, memory)

def reference(latent, control_latent, patch_tiles, tile_lists, tile_counts, embed_weight, control_embed, modulation, qk_gain, qkv_weight, out_weight, stale_cache, control_gain, final_mod, final_weight):
    row_count = PMAX * TILE
    padding = ((0, row_count), (0, 0))
    latent_pad = jnp.pad(latent, padding)
    control_pad = jnp.pad(control_latent, padding)
    memories = [jnp.pad(stale_cache[device_index], padding) for device_index in range(SLOTS * HG)]
    starts = jnp.cumsum(patch_tiles) - patch_tiles
    denoised = jnp.zeros((SEQ + row_count, C_OUT), jnp.float32)

    def apply_block(block_index, hidden, start_tile, patch_length):
        shifts = modulation[block_index]
        modded = modulated(hidden, shifts[0], shifts[1])
        summed = jnp.zeros((row_count, D), jnp.float32)
        for group_index in range(HG):
            device_index = block_index * HG + group_index
            partial_value, memories[device_index] = attend_group(modded, qkv_weight[device_index], out_weight[device_index], memories[device_index], qk_gain[block_index], start_tile, patch_length, tile_lists[block_index], tile_counts[block_index])
            rounded = lax.optimization_barrier(partial_value.astype(jnp.bfloat16))
            summed = summed + rounded.astype(jnp.float32)
        return hidden.astype(jnp.float32) + shifts[2] * summed
    for patch_index in range(PATCHES):
        start_tile = starts[patch_index]
        patch_length = patch_tiles[patch_index]
        row_start = (start_tile * TILE).astype(jnp.int32)
        own_latent = lax.dynamic_slice_in_dim(latent_pad, row_start, row_count, 0)
        own_control = lax.dynamic_slice_in_dim(control_pad, row_start, row_count, 0)
        embedded = jnp.dot(own_latent, embed_weight, preferred_element_type=jnp.float32)
        hidden = embedded.astype(jnp.bfloat16)
        control = (embedded + jnp.dot(own_control, control_embed, preferred_element_type=jnp.float32)).astype(jnp.bfloat16)
        for block_index in range(MAIN):
            control = apply_block(2 * block_index, control, start_tile, patch_length).astype(jnp.bfloat16)
            updated = apply_block(2 * block_index + 1, hidden, start_tile, patch_length)
            updated = updated + control_gain[block_index] * control.astype(jnp.float32)
            hidden = updated.astype(jnp.bfloat16)
        final_rows = jnp.dot(modulated(hidden, final_mod[0], final_mod[1]), final_weight, preferred_element_type=jnp.float32)
        previous = lax.dynamic_slice_in_dim(denoised, row_start, row_count, 0)
        live_rows = jnp.arange(row_count) < patch_length * TILE
        denoised = lax.dynamic_update_slice_in_dim(denoised, jnp.where(live_rows[:, None], final_rows, previous), row_start, 0)
    return denoised[:SEQ]
```

```python
import functools
import math

import jax
import jax.numpy as jnp
from jax import lax
from jax.experimental import pallas as pl
from jax.experimental.pallas import tpu as pltpu
from jax.sharding import PartitionSpec as P

HD = 128
HG = 8
TILE = 128
EPSILON = 1e-06
CHUNKS = 6
Y_FIRST = (True, True, False, True, True, False)
MESH = pl.DeviceIdType.MESH


def normed(values, shift_row, scale_row):
    centered = values - jnp.mean(values, axis=-1, keepdims=True)
    variance = jnp.mean(centered * centered, axis=-1, keepdims=True)
    return centered * lax.rsqrt(variance + EPSILON) * (1.0 + scale_row) + shift_row


def modulated(hidden, shift_row, scale_row):
    return normed(hidden.astype(jnp.float32), shift_row, scale_row).astype(jnp.bfloat16)


def rms_scaled(values, gain_row):
    return (
        values * lax.rsqrt(jnp.mean(values * values, axis=-1, keepdims=True) + EPSILON) * gain_row
    )


def attend_kernel(
    embeds,
    patch_tiles,
    tile_lists,
    tile_counts,
    modulation,
    qk_gain,
    w_qkv_hbm,
    stale_hbm,
    *rest,
):
    *sources, out, w_qkv, modded, queries, memory, w_sem, stale_sem = rest
    slot = lax.axis_index("section") // HG
    tiles = stale_hbm.shape[0]
    features = out.shape[1]
    heads = features // HD
    copies = []
    for part in range(3):
        columns = pl.ds(part * features, features)
        copies.append(
            pltpu.make_async_copy(
                w_qkv_hbm.at[:, columns], w_qkv.at[:, columns], w_sem.at[part]
            )
        )
        copies[-1].start()
    stale_copy = pltpu.make_async_copy(stale_hbm, memory.at[pl.ds(tiles, tiles)], stale_sem)
    stale_copy.start()

    for tile in range(tiles):
        rows = slice(tile * TILE, (tile + 1) * TILE)
        if embeds:
            latent, control_latent, embed_weight, control_embed = sources
            values = jnp.dot(
                latent[rows], embed_weight[...], preferred_element_type=jnp.float32
            ) + jnp.dot(
                control_latent[rows], control_embed[...], preferred_element_type=jnp.float32
            )
            values = values.astype(jnp.bfloat16)
        else:
            values = sources[0][rows]
        modded[rows] = modulated(values, modulation[slot, 0:1], modulation[slot, 1:2])

    for part in range(3):
        copies[part].wait()
        projected = jnp.dot(
            modded[...],
            w_qkv[:, part * features : (part + 1) * features],
            preferred_element_type=jnp.float32,
        )
        for head in range(heads):
            columns = slice(head * HD, (head + 1) * HD)
            values = projected[:, columns]
            if part < 2:
                values = rms_scaled(values, qk_gain[slot, part : part + 1])
            values = values.astype(jnp.bfloat16)
            if part == 0:
                queries[:, columns] = values
            else:
                offset = (part - 1) * features + head * HD
                memory[0:tiles, :, offset : offset + HD] = values.reshape(tiles, TILE, HD)
    stale_copy.wait()

    def patch_of(tile):
        end, patch = 0, 0
        for p in range(patch_tiles.shape[0]):
            end = end + patch_tiles[p]
            patch = patch + jnp.where(tile >= end, 1, 0)
        return patch

    for tile in range(tiles):
        rows = slice(tile * TILE, (tile + 1) * TILE)
        own_patch = patch_of(tile)
        listed = []
        for j in range(tile_lists.shape[2]):
            key_tile = tile_lists[slot, tile, j]
            listed.append(key_tile + jnp.where(patch_of(key_tile) <= own_patch, 0, tiles))
        used = tile_counts[slot, tile]
        for head in range(heads):
            columns = slice(head * HD, (head + 1) * HD)
            query = queries[rows, columns]
            scores = []
            for j, place in enumerate(listed):
                score = lax.dot_general(
                    query,
                    memory[place, :, columns],
                    (((1,), (1,)), ((), ())),
                    preferred_element_type=jnp.float32,
                ) / math.sqrt(HD)
                scores.append(jnp.where(j < used, score, -1e30))
            scores = jnp.concatenate(scores, axis=1)
            weights = jnp.exp(scores - jnp.max(scores, axis=-1, keepdims=True))
            probabilities = (weights / jnp.sum(weights, axis=-1, keepdims=True)).astype(
                jnp.bfloat16
            )
            value_columns = slice(features + head * HD, features + (head + 1) * HD)
            value_rows = jnp.concatenate([memory[place, :, value_columns] for place in listed])
            out[rows, columns] = jnp.dot(
                probabilities, value_rows, preferred_element_type=jnp.float32
            ).astype(jnp.bfloat16)


def attended_of(
    sources, patch_tiles, tile_lists, tile_counts, modulation, qk_gain, w_qkv, stale
):
    row_count, kv = stale.shape
    width, columns = w_qkv.shape
    tiles = row_count // TILE
    whole = pl.BlockSpec(memory_space=pltpu.VMEM)
    scalars = pl.BlockSpec(memory_space=pltpu.SMEM)
    far = pl.BlockSpec(memory_space=pl.ANY)
    return pl.pallas_call(
        functools.partial(attend_kernel, len(sources) == 4),
        out_shape=jax.ShapeDtypeStruct((row_count, kv // 2), jnp.bfloat16),
        in_specs=[scalars] * 3 + [whole] * 2 + [far] * 2 + [whole] * len(sources),
        out_specs=whole,
        scratch_shapes=[
            pltpu.VMEM((width, columns), jnp.bfloat16),
            pltpu.VMEM((row_count, width), jnp.bfloat16),
            pltpu.VMEM((row_count, kv // 2), jnp.bfloat16),
            pltpu.VMEM((2 * tiles, TILE, kv), jnp.bfloat16),
            pltpu.SemaphoreType.DMA((3,)),
            pltpu.SemaphoreType.DMA,
        ],
        compiler_params=pltpu.CompilerParams(vmem_limit_bytes=40 * 2**20),
        cost_estimate=pl.CostEstimate(
            flops=6 * 10**9, bytes_accessed=10**7, transcendentals=10**6
        ),
        name="attend",
    )(
        patch_tiles,
        tile_lists,
        tile_counts,
        modulation,
        qk_gain,
        w_qkv,
        stale.reshape(tiles, TILE, kv),
        *sources,
    )


def reduce_kernel(
    attended,
    w_out,
    modulation,
    control_gain,
    latent,
    control_latent,
    embed_weight,
    control_embed,
    tail,
    final_weight,
    out,
    contrib,
    total,
    gate,
    got0,
    got1,
    got2,
    got3,
    give1,
    give2,
    give3,
    send_sem,
    recv_sem,
):
    chunks = contrib.shape[0]
    share, width = contrib.shape[-2:]
    grp = lax.axis_index("grp")
    me = lax.axis_index("section")
    core, y_bit, z_bit, slot = me % 2, me // 2 % 2, me // 4 % 2, me // 8
    others = {
        "core": me + 1 - 2 * core,
        "y": me + 2 - 4 * y_bit,
        "z": me + 4 - 8 * z_bit,
        "slot": me + 8 - 16 * slot,
    }
    barrier = pltpu.get_barrier_semaphore()
    for other in others.values():
        pl.semaphore_signal(barrier, inc=1, device_id=(grp, other), device_id_type=MESH)
    gate[...] = modulation[slot, 2:3] * jnp.where(slot == 0, control_gain[0:1], 1.0)
    pl.semaphore_wait(barrier, 4)

    def exchange(stage, k, src, dst, other):
        return pltpu.make_async_remote_copy(
            src_ref=src,
            dst_ref=dst,
            send_sem=send_sem.at[stage, k],
            recv_sem=recv_sem.at[stage, k],
            device_id=(grp, other),
            device_id_type=MESH,
        )

    pending = {}

    def embedded(columns):
        plain = jnp.dot(
            latent[...], embed_weight[:, columns], preferred_element_type=jnp.float32
        )
        control = plain + jnp.dot(
            control_latent[...], control_embed[:, columns], preferred_element_type=jnp.float32
        )
        control = control.astype(jnp.bfloat16).astype(jnp.float32)
        return plain.astype(jnp.bfloat16).astype(jnp.float32) + control_gain[0:1, columns] * control

    def stage0(k):
        columns = slice(k * width, (k + 1) * width)
        part = jnp.dot(attended[...], w_out[:, columns], preferred_element_type=jnp.float32)
        part = (part * gate[:, columns]).astype(jnp.bfloat16)
        for block in range(16):
            s, zb, yb, c = block >> 3, block >> 2 & 1, block >> 1 & 1, block & 1
            first, second = (yb, zb) if Y_FIRST[k] else (zb, yb)
            contrib[k, c, first, second, s] = part[block * share : (block + 1) * share]
        pending[0, k] = exchange(0, k, contrib.at[k, 1 - core], got0.at[k], others["core"])
        pending[0, k].start()

    def later(stage, k):
        pending[stage - 1, k].wait()
        first, second = (y_bit, z_bit) if Y_FIRST[k] else (z_bit, y_bit)
        names = ("y", "z") if Y_FIRST[k] else ("z", "y")
        if stage == 1:
            for half, to in ((1 - first, give1.at[k]), (first, None)):
                summed = contrib[k, core, half].astype(jnp.float32) + got0[k, half].astype(
                    jnp.float32
                )
                if to is None:
                    contrib[k, core, half] = summed.astype(jnp.bfloat16)
                else:
                    to[...] = summed.astype(jnp.bfloat16)
                    pending[1, k] = exchange(1, k, to, got1.at[k], others[names[0]])
                    pending[1, k].start()
        elif stage == 2:
            for half, to in ((1 - second, give2.at[k]), (second, None)):
                summed = contrib[k, core, first, half].astype(jnp.float32) + got1[
                    k, half
                ].astype(jnp.float32)
                if to is None:
                    contrib[k, core, first, half] = summed.astype(jnp.bfloat16)
                else:
                    to[...] = summed.astype(jnp.bfloat16)
                    pending[2, k] = exchange(2, k, to, got2.at[k], others[names[1]])
                    pending[2, k].start()
        elif stage == 3:
            for half, to in ((1 - slot, give3.at[k]), (slot, None)):
                summed = contrib[k, core, first, second, half].astype(jnp.float32) + got2[
                    k, half
                ].astype(jnp.float32)
                if to is None:
                    columns = slice(k * width, (k + 1) * width)
                    total[:, columns] = summed + embedded(columns)
                else:
                    to[...] = summed.astype(jnp.bfloat16)
                    pending[3, k] = exchange(3, k, to, got3.at[k], others["slot"])
                    pending[3, k].start()
        else:
            columns = slice(k * width, (k + 1) * width)
            total[:, columns] = (
                total[:, columns] + got3[k].astype(jnp.float32)
            )

    for step in range(chunks + 4):
        for stage in range(4, 0, -1):
            if 0 <= step - stage < chunks:
                later(stage, step - stage)
        if step < chunks:
            stage0(step)

    hidden = total[...].astype(jnp.bfloat16).astype(jnp.float32)
    modded = normed(hidden, tail[0:1], tail[1:2]).astype(jnp.bfloat16)
    out[...] = jnp.dot(modded, final_weight[...], preferred_element_type=jnp.float32)


def reduced(
    attended,
    w_out,
    modulation,
    control_gain,
    latent,
    control_latent,
    embed_weight,
    control_embed,
    final_mod,
    final_weight,
):
    share, width = latent.shape[0], w_out.shape[1]
    cw = width // CHUNKS
    bf = jnp.bfloat16
    whole = pl.BlockSpec(memory_space=pltpu.VMEM)
    return pl.pallas_call(
        reduce_kernel,
        out_shape=jax.ShapeDtypeStruct((share, final_weight.shape[1]), jnp.float32),
        in_specs=[whole] * 10,
        out_specs=whole,
        scratch_shapes=[
            pltpu.VMEM((CHUNKS, 2, 2, 2, 2, share, cw), bf),
            pltpu.VMEM((share, width), jnp.float32),
            pltpu.VMEM((1, width), jnp.float32),
            pltpu.VMEM((CHUNKS, 2, 2, 2, share, cw), bf),
            pltpu.VMEM((CHUNKS, 2, 2, share, cw), bf),
            pltpu.VMEM((CHUNKS, 2, share, cw), bf),
            pltpu.VMEM((CHUNKS, share, cw), bf),
            pltpu.VMEM((CHUNKS, 2, 2, share, cw), bf),
            pltpu.VMEM((CHUNKS, 2, share, cw), bf),
            pltpu.VMEM((CHUNKS, share, cw), bf),
            pltpu.SemaphoreType.DMA((4, CHUNKS)),
            pltpu.SemaphoreType.DMA((4, CHUNKS)),
        ],
        compiler_params=pltpu.CompilerParams(
            collective_id=0, has_side_effects=True, vmem_limit_bytes=48 * 2**20
        ),
        cost_estimate=pl.CostEstimate(flops=2 * 10**9, bytes_accessed=10**7, transcendentals=0),
        name="reduce_rows",
    )(
        attended,
        w_out,
        modulation,
        control_gain,
        latent,
        control_latent,
        embed_weight,
        control_embed,
        final_mod,
        final_weight,
    )


def gathered(rows):
    me = lax.axis_index("section")
    count = lax.axis_size("section")
    step = 1
    while step < count:
        partner = lax.ppermute(rows, "section", [(i, i ^ step) for i in range(count)])
        upper = me // step % 2 == 1
        rows = jnp.concatenate(
            [jnp.where(upper, partner, rows), jnp.where(upper, rows, partner)]
        )
        step *= 2
    return rows


def embed(latent, control_latent, embed_weight, control_embed):
    embedded = jnp.dot(latent, embed_weight, preferred_element_type=jnp.float32)
    conditioned = embedded + jnp.dot(
        control_latent, control_embed, preferred_element_type=jnp.float32
    )
    return embedded.astype(jnp.bfloat16), conditioned.astype(jnp.bfloat16)


def on_device(
    latent,
    control_latent,
    patch_tiles,
    tile_lists,
    tile_counts,
    embed_weight,
    control_embed,
    modulation,
    qk_gain,
    qkv_weight,
    out_weight,
    stale_cache,
    control_gain,
    final_mod,
    final_weight,
):
    count = lax.axis_size("section")
    slot_count = count // HG
    me = lax.axis_index("section")
    slot = me // HG
    is_control = slot % 2 == 0
    def attended(*sources):
        return attended_of(
            sources,
            patch_tiles,
            tile_lists,
            tile_counts,
            modulation,
            qk_gain,
            qkv_weight[0],
            stale_cache[0],
        )

    if slot_count == 2:
        both = gathered(jnp.concatenate([latent, control_latent], axis=1))
        half = latent.shape[1]
        whole_latent, whole_control = both[:, :half], both[:, half:]
        used_control = jnp.where(is_control, whole_control, jnp.zeros_like(whole_control))
        return reduced(
            attended(whole_latent, used_control, embed_weight, control_embed),
            out_weight[0],
            modulation,
            control_gain,
            latent,
            control_latent,
            embed_weight,
            control_embed,
            final_mod,
            final_weight,
        )

    def level_of(level, own):
        own_hidden, own_control = own
        rows = jnp.where(
            is_control,
            lax.all_gather(own_control, "section", axis=0, tiled=True),
            lax.all_gather(own_hidden, "section", axis=0, tiled=True),
        )
        partial_value = jnp.dot(
            attended(rows), out_weight[0], preferred_element_type=jnp.float32
        ).astype(jnp.bfloat16)

        def summed(of_slot):
            masked = jnp.where(slot == of_slot, partial_value.astype(jnp.float32), 0.0)
            return modulation[of_slot, 2] * lax.psum_scatter(
                masked, "section", scatter_dimension=0, tiled=True
            )

        own_control = (own_control.astype(jnp.float32) + summed(2 * level)).astype(jnp.bfloat16)
        own_hidden = own_hidden.astype(jnp.float32) + summed(2 * level + 1)
        own_hidden = own_hidden + control_gain[level] * own_control.astype(jnp.float32)
        return own_hidden.astype(jnp.bfloat16), own_control

    own = embed(latent, control_latent, embed_weight, control_embed)
    own = lax.fori_loop(0, slot_count // 2, level_of, own)
    return jnp.dot(
        modulated(own[0], final_mod[0], final_mod[1]),
        final_weight,
        preferred_element_type=jnp.float32,
    )


def solution(mesh):
    return jax.shard_map(
        on_device,
        mesh=mesh,
        in_specs=(
            P(("grp", "section"), None),
            P(("grp", "section"), None),
            P(),
            P(),
            P(),
            P(),
            P(),
            P(),
            P(),
            P("section", None, None),
            P("section", None, None),
            P("section", "grp", None),
            P(),
            P(),
            P(),
        ),
        out_specs=P(("grp", "section"), None),
        check_vma=False,
    )
```

```python
import functools
import math

import jax
import jax.numpy as jnp
from jax import lax
from jax.experimental import pallas as pl
from jax.experimental.pallas import tpu as pltpu
from jax.sharding import PartitionSpec as P

HD = 128
HG = 8
TILE = 128
EPSILON = 1e-06
CHUNKS = 8
Y_FIRST = (True, True, False, True, True, False, True, True)
MESH = pl.DeviceIdType.MESH


def normed(values, shift_row, scale_row):
    centered = values - jnp.mean(values, axis=-1, keepdims=True)
    variance = jnp.mean(centered * centered, axis=-1, keepdims=True)
    return centered * lax.rsqrt(variance + EPSILON) * (1.0 + scale_row) + shift_row


def modulated(hidden, shift_row, scale_row):
    return normed(hidden.astype(jnp.float32), shift_row, scale_row).astype(jnp.bfloat16)


def rms_scaled(values, gain_row):
    return (
        values * lax.rsqrt(jnp.mean(values * values, axis=-1, keepdims=True) + EPSILON) * gain_row
    )


def attend_kernel(
    embeds,
    patch_tiles,
    tile_lists,
    tile_counts,
    modulation,
    qk_gain,
    w_qkv_hbm,
    stale_hbm,
    *rest,
):
    *sources, out, w_qkv, modded, queries, memory, w_sem, stale_sem = rest
    slot = lax.axis_index("section") // HG
    tiles = stale_hbm.shape[0]
    features = out.shape[1]
    heads = features // HD
    copies = []
    for part in range(3):
        columns = pl.ds(part * features, features)
        copies.append(
            pltpu.make_async_copy(
                w_qkv_hbm.at[:, columns], w_qkv.at[:, columns], w_sem.at[part]
            )
        )
        copies[-1].start()
    stale_copy = pltpu.make_async_copy(stale_hbm, memory.at[pl.ds(tiles, tiles)], stale_sem)
    stale_copy.start()

    for tile in range(tiles):
        rows = slice(tile * TILE, (tile + 1) * TILE)
        if embeds:
            latent, control_latent, embed_weight, control_embed = sources
            values = jnp.dot(
                latent[rows], embed_weight[...], preferred_element_type=jnp.float32
            ) + jnp.dot(
                control_latent[rows], control_embed[...], preferred_element_type=jnp.float32
            )
            values = values.astype(jnp.bfloat16)
        else:
            values = sources[0][rows]
        modded[rows] = modulated(values, modulation[slot, 0:1], modulation[slot, 1:2])

    for part in range(3):
        copies[part].wait()
        projected = jnp.dot(
            modded[...],
            w_qkv[:, part * features : (part + 1) * features],
            preferred_element_type=jnp.float32,
        )
        for head in range(heads):
            columns = slice(head * HD, (head + 1) * HD)
            values = projected[:, columns]
            if part < 2:
                values = rms_scaled(values, qk_gain[slot, part : part + 1])
            values = values.astype(jnp.bfloat16)
            if part == 0:
                queries[:, columns] = values
            else:
                offset = (part - 1) * features + head * HD
                memory[0:tiles, :, offset : offset + HD] = values.reshape(tiles, TILE, HD)
    stale_copy.wait()

    def patch_of(tile):
        end, patch = 0, 0
        for p in range(patch_tiles.shape[0]):
            end = end + patch_tiles[p]
            patch = patch + jnp.where(tile >= end, 1, 0)
        return patch

    for tile in range(tiles):
        rows = slice(tile * TILE, (tile + 1) * TILE)
        own_patch = patch_of(tile)
        listed = []
        for j in range(tile_lists.shape[2]):
            key_tile = tile_lists[slot, tile, j]
            listed.append(key_tile + jnp.where(patch_of(key_tile) <= own_patch, 0, tiles))
        used = tile_counts[slot, tile]
        for head in range(heads):
            columns = slice(head * HD, (head + 1) * HD)
            query = queries[rows, columns]
            scores = []
            for j, place in enumerate(listed):
                score = lax.dot_general(
                    query,
                    memory[place, :, columns],
                    (((1,), (1,)), ((), ())),
                    preferred_element_type=jnp.float32,
                ) / math.sqrt(HD)
                scores.append(jnp.where(j < used, score, -1e30))
            scores = jnp.concatenate(scores, axis=1)
            weights = jnp.exp(scores - jnp.max(scores, axis=-1, keepdims=True))
            probabilities = (weights / jnp.sum(weights, axis=-1, keepdims=True)).astype(
                jnp.bfloat16
            )
            value_columns = slice(features + head * HD, features + (head + 1) * HD)
            value_rows = jnp.concatenate([memory[place, :, value_columns] for place in listed])
            out[rows, columns] = jnp.dot(
                probabilities, value_rows, preferred_element_type=jnp.float32
            ).astype(jnp.bfloat16)


def attended_of(
    sources, patch_tiles, tile_lists, tile_counts, modulation, qk_gain, w_qkv, stale
):
    row_count, kv = stale.shape
    width, columns = w_qkv.shape
    tiles = row_count // TILE
    whole = pl.BlockSpec(memory_space=pltpu.VMEM)
    scalars = pl.BlockSpec(memory_space=pltpu.SMEM)
    far = pl.BlockSpec(memory_space=pl.ANY)
    return pl.pallas_call(
        functools.partial(attend_kernel, len(sources) == 4),
        out_shape=jax.ShapeDtypeStruct((row_count, kv // 2), jnp.bfloat16),
        in_specs=[scalars] * 3 + [whole] * 2 + [far] * 2 + [whole] * len(sources),
        out_specs=whole,
        scratch_shapes=[
            pltpu.VMEM((width, columns), jnp.bfloat16),
            pltpu.VMEM((row_count, width), jnp.bfloat16),
            pltpu.VMEM((row_count, kv // 2), jnp.bfloat16),
            pltpu.VMEM((2 * tiles, TILE, kv), jnp.bfloat16),
            pltpu.SemaphoreType.DMA((3,)),
            pltpu.SemaphoreType.DMA,
        ],
        compiler_params=pltpu.CompilerParams(vmem_limit_bytes=40 * 2**20),
        cost_estimate=pl.CostEstimate(
            flops=6 * 10**9, bytes_accessed=10**7, transcendentals=10**6
        ),
        name="attend",
    )(
        patch_tiles,
        tile_lists,
        tile_counts,
        modulation,
        qk_gain,
        w_qkv,
        stale.reshape(tiles, TILE, kv),
        *sources,
    )


def reduce_kernel(
    attended,
    w_out,
    modulation,
    control_gain,
    latent,
    control_latent,
    embed_weight,
    control_embed,
    tail,
    final_weight,
    out,
    contrib,
    total,
    gate,
    got0,
    got1,
    got2,
    got3,
    give1,
    give2,
    give3,
    send_sem,
    recv_sem,
):
    chunks = contrib.shape[0]
    share, width = contrib.shape[-2:]
    grp = lax.axis_index("grp")
    me = lax.axis_index("section")
    core, y_bit, z_bit, slot = me % 2, me // 2 % 2, me // 4 % 2, me // 8
    others = {
        "core": me + 1 - 2 * core,
        "y": me + 2 - 4 * y_bit,
        "z": me + 4 - 8 * z_bit,
        "slot": me + 8 - 16 * slot,
    }
    barrier = pltpu.get_barrier_semaphore()
    for other in others.values():
        pl.semaphore_signal(barrier, inc=1, device_id=(grp, other), device_id_type=MESH)
    gate[...] = modulation[slot, 2:3] * jnp.where(slot == 0, control_gain[0:1], 1.0)
    pl.semaphore_wait(barrier, 4)

    def exchange(stage, k, src, dst, other):
        return pltpu.make_async_remote_copy(
            src_ref=src,
            dst_ref=dst,
            send_sem=send_sem.at[stage, k],
            recv_sem=recv_sem.at[stage, k],
            device_id=(grp, other),
            device_id_type=MESH,
        )

    pending = {}

    def embedded(columns):
        plain = jnp.dot(
            latent[...], embed_weight[:, columns], preferred_element_type=jnp.float32
        )
        control = plain + jnp.dot(
            control_latent[...], control_embed[:, columns], preferred_element_type=jnp.float32
        )
        control = control.astype(jnp.bfloat16).astype(jnp.float32)
        return plain.astype(jnp.bfloat16).astype(jnp.float32) + control_gain[0:1, columns] * control

    def stage0(k):
        columns = slice(k * width, (k + 1) * width)
        part = jnp.dot(attended[...], w_out[:, columns], preferred_element_type=jnp.float32)
        part = (part * gate[:, columns]).astype(jnp.bfloat16)
        for block in range(16):
            s, zb, yb, c = block >> 3, block >> 2 & 1, block >> 1 & 1, block & 1
            first, second = (yb, zb) if Y_FIRST[k] else (zb, yb)
            contrib[k, c, first, second, s] = part[block * share : (block + 1) * share]
        pending[0, k] = exchange(0, k, contrib.at[k, 1 - core], got0.at[k], others["core"])
        pending[0, k].start()

    def later(stage, k):
        pending[stage - 1, k].wait()
        first, second = (y_bit, z_bit) if Y_FIRST[k] else (z_bit, y_bit)
        names = ("y", "z") if Y_FIRST[k] else ("z", "y")
        if stage == 1:
            for half, to in ((1 - first, give1.at[k]), (first, None)):
                summed = contrib[k, core, half].astype(jnp.float32) + got0[k, half].astype(
                    jnp.float32
                )
                if to is None:
                    contrib[k, core, half] = summed.astype(jnp.bfloat16)
                else:
                    to[...] = summed.astype(jnp.bfloat16)
                    pending[1, k] = exchange(1, k, to, got1.at[k], others[names[0]])
                    pending[1, k].start()
        elif stage == 2:
            for half, to in ((1 - second, give2.at[k]), (second, None)):
                summed = contrib[k, core, first, half].astype(jnp.float32) + got1[
                    k, half
                ].astype(jnp.float32)
                if to is None:
                    contrib[k, core, first, half] = summed.astype(jnp.bfloat16)
                else:
                    to[...] = summed.astype(jnp.bfloat16)
                    pending[2, k] = exchange(2, k, to, got2.at[k], others[names[1]])
                    pending[2, k].start()
        elif stage == 3:
            for half, to in ((1 - slot, give3.at[k]), (slot, None)):
                summed = contrib[k, core, first, second, half].astype(jnp.float32) + got2[
                    k, half
                ].astype(jnp.float32)
                if to is None:
                    columns = slice(k * width, (k + 1) * width)
                    total[:, columns] = summed + embedded(columns)
                else:
                    to[...] = summed.astype(jnp.bfloat16)
                    pending[3, k] = exchange(3, k, to, got3.at[k], others["slot"])
                    pending[3, k].start()
        else:
            columns = slice(k * width, (k + 1) * width)
            total[:, columns] = (
                total[:, columns] + got3[k].astype(jnp.float32)
            )

    for step in range(chunks + 4):
        for stage in range(4, 0, -1):
            if 0 <= step - stage < chunks:
                later(stage, step - stage)
        if step < chunks:
            stage0(step)

    hidden = total[...].astype(jnp.bfloat16).astype(jnp.float32)
    modded = normed(hidden, tail[0:1], tail[1:2]).astype(jnp.bfloat16)
    out[...] = jnp.dot(modded, final_weight[...], preferred_element_type=jnp.float32)


def reduced(
    attended,
    w_out,
    modulation,
    control_gain,
    latent,
    control_latent,
    embed_weight,
    control_embed,
    final_mod,
    final_weight,
):
    share, width = latent.shape[0], w_out.shape[1]
    cw = width // CHUNKS
    bf = jnp.bfloat16
    whole = pl.BlockSpec(memory_space=pltpu.VMEM)
    return pl.pallas_call(
        reduce_kernel,
        out_shape=jax.ShapeDtypeStruct((share, final_weight.shape[1]), jnp.float32),
        in_specs=[whole] * 10,
        out_specs=whole,
        scratch_shapes=[
            pltpu.VMEM((CHUNKS, 2, 2, 2, 2, share, cw), bf),
            pltpu.VMEM((share, width), jnp.float32),
            pltpu.VMEM((1, width), jnp.float32),
            pltpu.VMEM((CHUNKS, 2, 2, 2, share, cw), bf),
            pltpu.VMEM((CHUNKS, 2, 2, share, cw), bf),
            pltpu.VMEM((CHUNKS, 2, share, cw), bf),
            pltpu.VMEM((CHUNKS, share, cw), bf),
            pltpu.VMEM((CHUNKS, 2, 2, share, cw), bf),
            pltpu.VMEM((CHUNKS, 2, share, cw), bf),
            pltpu.VMEM((CHUNKS, share, cw), bf),
            pltpu.SemaphoreType.DMA((4, CHUNKS)),
            pltpu.SemaphoreType.DMA((4, CHUNKS)),
        ],
        compiler_params=pltpu.CompilerParams(
            collective_id=0, has_side_effects=True, vmem_limit_bytes=48 * 2**20
        ),
        cost_estimate=pl.CostEstimate(flops=2 * 10**9, bytes_accessed=10**7, transcendentals=0),
        name="reduce_rows",
    )(
        attended,
        w_out,
        modulation,
        control_gain,
        latent,
        control_latent,
        embed_weight,
        control_embed,
        final_mod,
        final_weight,
    )


def gathered(rows):
    me = lax.axis_index("section")
    count = lax.axis_size("section")
    step = 1
    while step < count:
        partner = lax.ppermute(rows, "section", [(i, i ^ step) for i in range(count)])
        upper = me // step % 2 == 1
        rows = jnp.concatenate(
            [jnp.where(upper, partner, rows), jnp.where(upper, rows, partner)]
        )
        step *= 2
    return rows


def embed(latent, control_latent, embed_weight, control_embed):
    embedded = jnp.dot(latent, embed_weight, preferred_element_type=jnp.float32)
    conditioned = embedded + jnp.dot(
        control_latent, control_embed, preferred_element_type=jnp.float32
    )
    return embedded.astype(jnp.bfloat16), conditioned.astype(jnp.bfloat16)


def on_device(
    latent,
    control_latent,
    patch_tiles,
    tile_lists,
    tile_counts,
    embed_weight,
    control_embed,
    modulation,
    qk_gain,
    qkv_weight,
    out_weight,
    stale_cache,
    control_gain,
    final_mod,
    final_weight,
):
    count = lax.axis_size("section")
    slot_count = count // HG
    me = lax.axis_index("section")
    slot = me // HG
    is_control = slot % 2 == 0
    def attended(*sources):
        return attended_of(
            sources,
            patch_tiles,
            tile_lists,
            tile_counts,
            modulation,
            qk_gain,
            qkv_weight[0],
            stale_cache[0],
        )

    if slot_count == 2:
        both = gathered(jnp.concatenate([latent, control_latent], axis=1))
        half = latent.shape[1]
        whole_latent, whole_control = both[:, :half], both[:, half:]
        used_control = jnp.where(is_control, whole_control, jnp.zeros_like(whole_control))
        return reduced(
            attended(whole_latent, used_control, embed_weight, control_embed),
            out_weight[0],
            modulation,
            control_gain,
            latent,
            control_latent,
            embed_weight,
            control_embed,
            final_mod,
            final_weight,
        )

    def level_of(level, own):
        own_hidden, own_control = own
        rows = jnp.where(
            is_control,
            lax.all_gather(own_control, "section", axis=0, tiled=True),
            lax.all_gather(own_hidden, "section", axis=0, tiled=True),
        )
        partial_value = jnp.dot(
            attended(rows), out_weight[0], preferred_element_type=jnp.float32
        ).astype(jnp.bfloat16)

        def summed(of_slot):
            masked = jnp.where(slot == of_slot, partial_value.astype(jnp.float32), 0.0)
            return modulation[of_slot, 2] * lax.psum_scatter(
                masked, "section", scatter_dimension=0, tiled=True
            )

        own_control = (own_control.astype(jnp.float32) + summed(2 * level)).astype(jnp.bfloat16)
        own_hidden = own_hidden.astype(jnp.float32) + summed(2 * level + 1)
        own_hidden = own_hidden + control_gain[level] * own_control.astype(jnp.float32)
        return own_hidden.astype(jnp.bfloat16), own_control

    own = embed(latent, control_latent, embed_weight, control_embed)
    own = lax.fori_loop(0, slot_count // 2, level_of, own)
    return jnp.dot(
        modulated(own[0], final_mod[0], final_mod[1]),
        final_weight,
        preferred_element_type=jnp.float32,
    )


def solution(mesh):
    return jax.shard_map(
        on_device,
        mesh=mesh,
        in_specs=(
            P(("grp", "section"), None),
            P(("grp", "section"), None),
            P(),
            P(),
            P(),
            P(),
            P(),
            P(),
            P(),
            P("section", None, None),
            P("section", None, None),
            P("section", "grp", None),
            P(),
            P(),
            P(),
        ),
        out_specs=P(("grp", "section"), None),
        check_vma=False,
    )
```
